32 devices in a mesh: grp: 8 (over y, x, core), tp: 4 (over z).
Axes of the slice: x: 2, y: 2, z: 4, core: 2. Of those that a mesh axis runs over, the one named last changes fastest.
Arguments:
- sel_hidden: bfloat16 [16, 320, 4096], P('grp'), may hold values from -6 to 6
- norm_gain: float32 [4096], replicated, may hold values from 0.25 to 1.75
- w_query: bfloat16 [4096, 4096], P(None, 'tp'), may hold values from -0.09375 to 0.09375
- w_key: bfloat16 [4096, 1024], P(None, 'tp'), may hold values from -0.1875 to 0.1875
- w_value: bfloat16 [4096, 1024], P(None, 'tp'), may hold values from -0.09375 to 0.09375
- w_out: bfloat16 [4096, 4096], P(None, 'tp'), may hold values from -0.09375 to 0.09375
- doc_cache: bfloat16 [128, 2, 512, 1024], P('grp', None, None, 'tp'), may hold values from -250 to 250
- home: int32 [128], replicated, may hold values from 0 to 127, as said below
- doc_ids: int32 [16, 8], replicated, may hold values from 0 to 127, as said below
- doc_len: int32 [128], replicated, may hold values from 128 to 512, as said below
- positions: int32 [16, 320], P('grp'), may hold values from 0 to 4095, as said below
Outputs:
- mixed: bfloat16 [16, 320, 4096], P('grp', None, 'tp')
The draws below stay inside these ranges and needn't reach their ends.
Inputs may be any that keep to these rules, and one draw needn't show every extreme that they name: `home`: a permutation: every location holds one document; the owner of location l along grp is l // 16. `doc_ids`: requests g * 2 .. (g + 1) * 2 - 1 form serving group g; the 16 documents of one group all differ, no owner holds more than 2 of them, and in every group at least one owner holds exactly 2. `doc_len`: documents doc_ids[0, 0] and doc_ids[0, 7] have length 512 (others may too). positions: each row rises; for each j it holds 40 positions j * 512 + t with t below the length of document doc_ids[r, j].
All inputs are finite; a program needn't handle non-finite values.
Results may differ from the reference program's by a relative error of at most 0.006.
The reference program's roundings to bfloat16 on the way (of `normed`, `weights` and `attn`) count: a program that leaves them out, or rounds other values in their place, can miss the bound.
Values may be sent and summed in bfloat16 or wider, within the bound.
A program may use at most 192 MiB of HBM per device.

```python
import jax
import jax.numpy as jnp
from jax import lax

D = 4096
H = 32
KVH = 8
HD = 128
R_DOCS = 8
DOC_LEN = 512
CAP = 2
REQ_GRP = 2
PICK = 40
DOC_DEV = 16
RECOMP = 320
REQS = 16
DOCS = 128


def plan_tables(key):
    keys = jax.random.split(key, 8)
    groups = REQS // REQ_GRP
    per_group = REQ_GRP * R_DOCS
    home = jax.random.permutation(keys[0], DOCS).astype(jnp.int32)
    resident = jnp.argsort(home).astype(jnp.int32)
    first = jax.random.randint(keys[1], (groups,), 0, groups)
    spread = (groups - 1) * CAP
    tickets = jax.random.randint(keys[2], (groups, spread), 0, 2 ** 20) * spread + jnp.arange(spread)[None, :]
    order = jnp.argsort(tickets, axis=1)[:, :per_group - CAP]
    others = (first[:, None] + 1 + order // CAP) % groups
    owners = jnp.concatenate([jnp.broadcast_to(first[:, None], (groups, CAP)), others], axis=1)
    within = jnp.concatenate([jnp.broadcast_to(jnp.arange(CAP)[None, :], (groups, CAP)), order % CAP], axis=1)
    span = DOC_DEV // CAP
    lower = jnp.minimum(jax.random.randint(keys[3], (groups, per_group), 0, span), jax.random.randint(keys[4], (groups, per_group), 0, span))
    location = owners * DOC_DEV + within * span + lower
    shuffle = jnp.argsort(jax.random.randint(keys[5], (groups, per_group), 0, 2 ** 20) * per_group + jnp.arange(per_group)[None, :], axis=1)
    location = jnp.take_along_axis(location, shuffle, axis=1).reshape(REQS, R_DOCS)
    doc_ids = resident[location].astype(jnp.int32)
    lengths = jax.random.randint(keys[6], (DOCS,), DOC_LEN // 4, DOC_LEN + 1)
    lengths = lengths.at[doc_ids[0, 0]].set(DOC_LEN)
    lengths = lengths.at[doc_ids[0, R_DOCS - 1]].set(DOC_LEN)
    lengths = lengths.at[doc_ids[0, 1]].set(DOC_LEN // 4).astype(jnp.int32)
    own_len = lengths[doc_ids]
    offsets = jnp.arange(DOC_LEN)
    marks = jax.random.randint(keys[7], (REQS, R_DOCS, DOC_LEN), 0, 2 ** 20) * DOC_LEN + offsets
    marks = jnp.where(offsets[None, None, :] < own_len[:, :, None], marks, 2 ** 30)
    req_ix = jnp.arange(REQS)[:, None, None]
    doc_ix = jnp.arange(R_DOCS)[None, :, None]
    off_ix = offsets[None, None, :]
    forced = (req_ix == 0) & ((doc_ix == 0) & (off_ix == 0) | (doc_ix == R_DOCS - 1) & (off_ix == DOC_LEN - 1))
    marks = jnp.where(forced, -1, marks)
    picked = jnp.sort(jnp.argsort(marks, axis=2)[:, :, :PICK], axis=2)
    rows = (picked + jnp.arange(R_DOCS)[None, :, None] * DOC_LEN).reshape(REQS, RECOMP).astype(jnp.int32)
    return (home, doc_ids, lengths, rows)


def draw_home(key, part):
    return plan_tables(key)[0]


def draw_doc_ids(key, part):
    return plan_tables(key)[1]


def draw_doc_len(key, part):
    return plan_tables(key)[2]


def draw_positions(key, part):
    return plan_tables(key)[3]


def draw_doc_cache(key, part):
    key = jax.random.fold_in(key, 11)
    key_k, key_v = jax.random.split(key, 2)
    shape = (DOCS, DOC_LEN, KVH * HD)
    cached_keys = jnp.clip(2.0 * jax.random.normal(key_k, shape), -12.0, 12.0)
    cached_values = jnp.clip(jax.random.normal(key_v, shape), -6.0, 6.0)
    return jnp.stack([cached_keys, cached_values], axis=1).astype(jnp.bfloat16)


def shard_levels(key, shape, pieces, least, high):
    loudness, own = 1.0, jax.random.fold_in(key, 6)
    for axis_at, blocks in pieces:
        steps = jnp.exp(jax.random.uniform(jax.random.fold_in(own, axis_at), (blocks,), jnp.float32, least / len(pieces), high / len(pieces)))
        loudness = loudness * jnp.repeat(steps, shape[axis_at] // blocks).reshape([-1 if axis == axis_at else 1 for axis in range(len(shape))])
    return loudness


def gaussian(own_key, dims, deviation, bound, cuts=(), held_as=jnp.bfloat16):
    entries = deviation * jax.random.normal(own_key, dims, jnp.float32)
    if cuts:
        entries = entries * shard_levels(own_key, dims, cuts, -0.22, 0.18)
    return jnp.clip(entries, -bound, bound).astype(held_as)


def setup_inputs(seed: int = 0) -> dict:
    splits = jax.random.split(jax.random.key(seed), 12)
    sel_hidden = gaussian(splits[0], (REQS, RECOMP, D), 1.0, 6.0, ((0, 8),))
    norm_gain = jnp.clip(1.0 + 0.15 * jax.random.normal(splits[1], (D,), jnp.float32), 0.25, 1.75)
    w_query = gaussian(splits[2], (D, H * HD), D ** -0.5, 0.09375, ((1, 4),))
    w_key = gaussian(splits[3], (D, KVH * HD), (D // 4) ** -0.5, 0.1875, ((1, 4),))
    w_value = gaussian(splits[4], (D, KVH * HD), D ** -0.5, 0.09375, ((1, 4),))
    w_out = gaussian(splits[5], (H * HD, D), (H * HD) ** -0.5, 0.09375, ((1, 4),))
    doc_cache = draw_doc_cache(jax.random.fold_in(splits[11], 71), 0)
    home = draw_home(jax.random.fold_in(splits[11], 71), 0)
    doc_ids = draw_doc_ids(jax.random.fold_in(splits[11], 71), 0)
    doc_len = draw_doc_len(jax.random.fold_in(splits[11], 71), 0)
    positions = draw_positions(jax.random.fold_in(splits[11], 71), 0)
    return dict(sel_hidden=sel_hidden, norm_gain=norm_gain, w_query=w_query, w_key=w_key, w_value=w_value, w_out=w_out, doc_cache=doc_cache, home=home, doc_ids=doc_ids, doc_len=doc_len, positions=positions)


def reference(sel_hidden, norm_gain, w_query, w_key, w_value, w_out, doc_cache, home, doc_ids, doc_len, positions):
    group = H // KVH
    scale = HD ** (-0.5)

    def one_request(items):
        hidden, ids, where_rows = items
        xf = hidden.astype(jnp.float32)
        normed = (xf * lax.rsqrt(lax.optimization_barrier(jnp.mean(xf * xf, axis=-1, keepdims=True)) + 1e-05) * norm_gain).astype(jnp.bfloat16)
        query = jnp.dot(normed, w_query, preferred_element_type=jnp.float32).astype(jnp.bfloat16)
        key_new = jnp.dot(normed, w_key, preferred_element_type=jnp.float32).astype(jnp.bfloat16)
        value_new = jnp.dot(normed, w_value, preferred_element_type=jnp.float32).astype(jnp.bfloat16)
        context = doc_cache[home[ids]]
        keys_ctx = context[:, 0].reshape(R_DOCS * DOC_LEN, KVH * HD).at[where_rows].set(key_new)
        values_ctx = context[:, 1].reshape(R_DOCS * DOC_LEN, KVH * HD).at[where_rows].set(value_new)
        lengths = doc_len[ids]
        valid = (jnp.arange(DOC_LEN, dtype=jnp.int32)[None, :] < lengths[:, None]).reshape(R_DOCS * DOC_LEN)
        visible = valid[None, :] & (jnp.arange(R_DOCS * DOC_LEN, dtype=jnp.int32)[None, :] <= where_rows[:, None])

        def one_head(head):
            keys_h = lax.dynamic_slice_in_dim(keys_ctx, head * HD, HD, 1).astype(jnp.float32)
            values_h = lax.dynamic_slice_in_dim(values_ctx, head * HD, HD, 1).astype(jnp.float32)
            query_h = lax.dynamic_slice_in_dim(query, head * group * HD, group * HD, 1).reshape(RECOMP, group, HD).astype(jnp.float32)
            scores = jnp.einsum('qgd,kd->gqk', query_h, keys_h) * scale
            scores = jnp.where(visible[None], scores, -1e+30)
            top = lax.optimization_barrier(jnp.max(scores, axis=-1, keepdims=True))
            expo = jnp.exp(scores - top)
            weights = (expo / lax.optimization_barrier(jnp.sum(expo, axis=-1, keepdims=True))).astype(jnp.bfloat16)
            attn = jnp.einsum('gqk,kd->qgd', weights.astype(jnp.float32), values_h).astype(jnp.bfloat16)
            return attn.reshape(RECOMP, group * HD)
        heads = lax.map(one_head, jnp.arange(KVH, dtype=jnp.int32))
        attn_all = jnp.transpose(heads, (1, 0, 2)).reshape(RECOMP, H * HD)
        return jnp.dot(attn_all, w_out, preferred_element_type=jnp.float32).astype(jnp.bfloat16)
    return lax.map(one_request, (sel_hidden, doc_ids, positions))
```

```python
import functools

import jax
import jax.numpy as jnp
from jax import lax
from jax.experimental import pallas as pl
from jax.experimental.pallas import tpu as pltpu
from jax.sharding import PartitionSpec as P

H = 32
KVH = 8
HD = 128
CAP = 2
PAIR = 2
LANES = 128
MASKED = -1e30
LOG2E = 1.4426950408889634


def attention_kernel(retrieved, doc_rows, tokens, slots, lens, *refs):
    docs = refs[:retrieved]
    q_ref, new_k, new_v, pos_lane, pos_col, o_ref = refs[retrieved : retrieved + 6]
    keys, values, scores, top, total, acc = refs[retrieved + 6 :]
    group = H // KVH
    picks = tokens // retrieved
    span = PAIR * picks
    factor = HD ** (-0.5) * LOG2E
    request = pl.program_id(0)
    block = pl.program_id(1)

    @pl.when(block == 0)
    def blend():
        for j in range(retrieved):
            low = j * picks // LANES * LANES
            high = min(tokens, -(-(j + 1) * picks // LANES) * LANES)
            at = lax.broadcasted_iota(jnp.int32, (doc_rows, high - low), 0) + j * doc_rows
            hit = jnp.where(at == pos_lane[0, :, low:high], 1.0, 0.0).astype(jnp.bfloat16)
            ones = jnp.ones((high - low, HD), jnp.bfloat16)
            fresh = jnp.concatenate([new_k[low:high, :], new_v[low:high, :], ones], axis=1)
            placed = jnp.dot(hit, fresh, preferred_element_type=jnp.float32)
            replaced = placed[:, 2 * HD :] > 0.5
            keys[j] = jnp.where(
                replaced, placed[:, :HD], docs[j][0, 0].astype(jnp.float32)
            ).astype(jnp.bfloat16)
            values[j] = jnp.where(
                replaced, placed[:, HD : 2 * HD], docs[j][0, 1].astype(jnp.float32)
            ).astype(jnp.bfloat16)

    query = jnp.concatenate([q_ref[:, g * HD : (g + 1) * HD] for g in range(group)], axis=0)
    top[...] = jnp.full_like(top, MASKED)
    total[...] = jnp.zeros_like(total)
    acc[...] = jnp.zeros_like(acc)

    def score(j, mask_of):
        raw = lax.dot_general(
            query, keys[j], (((1,), (1,)), ((), ())), preferred_element_type=jnp.float32
        )
        mask = mask_of(j)
        for g in range(group):
            rows = slice(g * span, (g + 1) * span)
            part = jnp.where(mask, raw[rows, :], MASKED)
            scores[j, rows, :] = part
            best = top[rows, :]
            for n in range(doc_rows // LANES):
                best = jnp.maximum(best, part[:, n * LANES : (n + 1) * LANES])
            top[rows, :] = best

    def mask_full(j):
        length = lens[request * retrieved + j]
        return lax.broadcasted_iota(jnp.int32, (1, doc_rows), 1) < length

    def mask_diagonal(j):
        length = lens[request * retrieved + j]
        limit = jnp.minimum(pos_col[...] - j * doc_rows, length - 1)
        return lax.broadcasted_iota(jnp.int32, (span, doc_rows), 1) <= limit

    first = block * PAIR
    last = first + PAIR

    @pl.loop(0, first)
    def _(j):
        score(j, mask_full)

    for n in range(PAIR):
        score(first + n, mask_diagonal)

    peak = jnp.max(top[...], axis=1, keepdims=True) * factor
    top[...] = jnp.broadcast_to(peak, top.shape)

    @pl.loop(0, last)
    def _(j):
        for g in range(group):
            rows = slice(g * span, (g + 1) * span)
            shift = top[rows, :]
            add = total[rows, :]
            for n in range(doc_rows // LANES):
                cols = slice(n * LANES, (n + 1) * LANES)
                expo = jnp.exp2(scores[j, rows, cols] * factor - shift)
                scores[j, rows, cols] = expo
                add = add + expo
            total[rows, :] = add

    inverse = 1.0 / jnp.sum(total[...], axis=1, keepdims=True)
    total[...] = jnp.broadcast_to(inverse, total.shape)

    @pl.loop(0, last)
    def _(j):
        scale = total[...]
        weights = jnp.concatenate(
            [
                (scores[j, :, n * LANES : (n + 1) * LANES] * scale).astype(jnp.bfloat16)
                for n in range(doc_rows // LANES)
            ],
            axis=1,
        )
        acc[...] += jnp.dot(weights, values[j], preferred_element_type=jnp.float32)

    for g in range(group):
        o_ref[:, g * HD : (g + 1) * HD] = acc[g * span : (g + 1) * span, :].astype(o_ref.dtype)


def attention(head, cache, slots, lens, query, key_new, value_new, positions):
    served, tokens = positions.shape
    retrieved = slots.shape[0] // served
    doc_rows = cache.shape[2]
    group = H // KVH
    span = tokens // retrieved * PAIR
    blocks = retrieved // PAIR
    rows = group * span
    doc_specs = [
        pl.BlockSpec(
            (1, 2, doc_rows, HD),
            lambda r, b, slots, lens, j=j: (slots[r * retrieved + j], 0, 0, 0),
        )
        for j in range(retrieved)
    ]
    pairs = served * tokens * group * retrieved * doc_rows * 5 // 8
    return pl.pallas_call(
        functools.partial(attention_kernel, retrieved, doc_rows, tokens),
        grid_spec=pltpu.PrefetchScalarGridSpec(
            num_scalar_prefetch=2,
            grid=(served, blocks),
            in_specs=doc_specs
            + [
                pl.BlockSpec((span, group * HD), lambda r, b, *_: (r * blocks + b, head)),
                pl.BlockSpec((tokens, HD), lambda r, b, *_: (r, head)),
                pl.BlockSpec((tokens, HD), lambda r, b, *_: (r, head)),
                pl.BlockSpec((1, 1, tokens), lambda r, b, *_: (r, 0, 0)),
                pl.BlockSpec((span, 1), lambda r, b, *_: (r * blocks + b, 0)),
            ],
            out_specs=pl.BlockSpec((span, group * HD), lambda r, b, *_: (r * blocks + b, 0)),
            scratch_shapes=[
                pltpu.VMEM((retrieved, doc_rows, HD), jnp.bfloat16),
                pltpu.VMEM((retrieved, doc_rows, HD), jnp.bfloat16),
                pltpu.VMEM((retrieved, rows, doc_rows), jnp.float32),
                pltpu.VMEM((rows, LANES), jnp.float32),
                pltpu.VMEM((rows, LANES), jnp.float32),
                pltpu.VMEM((rows, HD), jnp.float32),
            ],
        ),
        out_shape=jax.ShapeDtypeStruct((served * tokens, group * HD), jnp.bfloat16),
        compiler_params=pltpu.CompilerParams(vmem_limit_bytes=40 * 2**20),
        cost_estimate=pl.CostEstimate(
            flops=8 * pairs * HD,
            bytes_accessed=2 * served * retrieved * doc_rows * 2 * HD,
            transcendentals=pairs,
        ),
    )(
        slots,
        lens,
        *([cache] * retrieved),
        query,
        key_new,
        value_new,
        positions[:, None, :],
        positions.reshape(served * tokens, 1),
    )


def body(
    sel_hidden,
    norm_gain,
    w_query,
    w_key,
    w_value,
    w_out,
    doc_cache,
    home,
    doc_ids,
    doc_len,
    positions,
):
    groups = lax.axis_size("grp")
    me = lax.axis_index("grp")
    stored = doc_cache.shape[0]
    doc_rows = doc_cache.shape[2]
    width = doc_cache.shape[3]
    kv_local = width // HD
    group = H // KVH
    served = sel_hidden.shape[0]
    tokens = sel_hidden.shape[1]
    retrieved = doc_ids.shape[1]
    per_group = served * retrieved
    location = home[doc_ids].reshape(groups, per_group)
    owner = location // stored
    slot_index = location % stored
    slots = jnp.arange(per_group, dtype=jnp.int32)
    earlier = (owner[:, :, None] == owner[:, None, :]) & (
        slots[None, None, :] < slots[None, :, None]
    )
    rank = jnp.sum(earlier.astype(jnp.int32), axis=2)
    match = (owner == me)[:, :, None] & (
        rank[:, :, None] == jnp.arange(CAP, dtype=jnp.int32)[None, None, :]
    )
    chosen = jnp.sum(jnp.where(match, slot_index[:, :, None], 0), axis=1)
    own_slots = owner[me] * CAP + rank[me]
    lengths = doc_len[doc_ids.reshape(groups, per_group)[me]]

    incoming = []
    for head in range(kv_local):
        outgoing = doc_cache[:, :, :, head * HD : (head + 1) * HD][chosen]
        if incoming:
            outgoing, incoming[-1] = lax.optimization_barrier((outgoing, incoming[-1]))
        incoming.append(
            lax.all_to_all(outgoing, "grp", split_axis=0, concat_axis=0, tiled=True)
        )

    xf = sel_hidden.astype(jnp.float32)
    normed = (xf * lax.rsqrt(jnp.mean(xf * xf, axis=-1, keepdims=True) + 1e-05) * norm_gain).astype(
        jnp.bfloat16
    )
    normed_rows = normed.reshape(served * tokens, normed.shape[2])
    query = jnp.dot(normed_rows, w_query, preferred_element_type=jnp.float32).astype(jnp.bfloat16)
    key_new = jnp.dot(normed_rows, w_key, preferred_element_type=jnp.float32).astype(jnp.bfloat16)
    value_new = jnp.dot(normed_rows, w_value, preferred_element_type=jnp.float32).astype(
        jnp.bfloat16
    )

    w_heads = w_out.reshape(-1, kv_local, group * HD, w_out.shape[1])
    mixed = 0.0
    for head in range(kv_local):
        cache = incoming[head].reshape((groups * CAP, 2, doc_rows, HD))
        attn = attention(
            head, cache, own_slots, lengths, query, key_new, value_new, positions
        )
        gathered = lax.all_gather(attn, "tp", axis=1, tiled=True)
        part = w_heads[:, head].reshape(-1, w_out.shape[1])
        mixed = mixed + jnp.dot(gathered, part, preferred_element_type=jnp.float32)
    return mixed.astype(jnp.bfloat16).reshape(served, tokens, w_out.shape[1])


def solution(mesh):
    return jax.shard_map(
        body,
        mesh=mesh,
        in_specs=(
            P("grp", None, None),
            P(),
            P(None, "tp"),
            P(None, "tp"),
            P(None, "tp"),
            P(None, "tp"),
            P("grp", None, None, "tp"),
            P(),
            P(),
            P(),
            P("grp", None),
        ),
        out_specs=P("grp", None, "tp"),
        check_vma=False,
    )
```

```python
import functools

import jax
import jax.numpy as jnp
from jax import lax
from jax.experimental import pallas as pl
from jax.experimental.pallas import tpu as pltpu
from jax.sharding import PartitionSpec as P

H = 32
KVH = 8
HD = 128
CAP = 2
PAIR = 2
LANES = 128
MASKED = -1e30
LOG2E = 1.4426950408889634


def pick_kernel(chosen, cache, out):
    out[...] = cache[...]


def pick(head, chosen, doc_cache):
    doc_rows = doc_cache.shape[2]
    count = chosen.shape[0]
    return pl.pallas_call(
        pick_kernel,
        grid_spec=pltpu.PrefetchScalarGridSpec(
            num_scalar_prefetch=1,
            grid=(count,),
            in_specs=[pl.BlockSpec((1, 2, doc_rows, HD), lambda i, chosen: (chosen[i], 0, 0, head))],
            out_specs=pl.BlockSpec((1, 2, doc_rows, HD), lambda i, chosen: (i, 0, 0, 0)),
        ),
        out_shape=jax.ShapeDtypeStruct((count, 2, doc_rows, HD), doc_cache.dtype),
        compiler_params=pltpu.CompilerParams(vmem_limit_bytes=32 * 2**20),
        cost_estimate=pl.CostEstimate(
            flops=0, bytes_accessed=8 * count * doc_rows * HD, transcendentals=0
        ),
    )(chosen, doc_cache)


def place_kernel(retrieved, doc_rows, new_k, new_v, pos_lane, keep, *placed):
    tokens = new_k.shape[0]
    picks = tokens // retrieved
    for j in range(retrieved):
        low = j * picks // LANES * LANES
        high = min(tokens, -(-(j + 1) * picks // LANES) * LANES)
        at = lax.broadcasted_iota(jnp.int32, (doc_rows, high - low), 0) + j * doc_rows
        hit = jnp.where(at == pos_lane[0, :, low:high], 1.0, 0.0).astype(jnp.bfloat16)
        ones = jnp.ones((high - low, HD), jnp.bfloat16)
        taken = jnp.dot(hit, ones, preferred_element_type=jnp.float32)
        keep[j] = (1.0 - taken).astype(jnp.bfloat16)
        for head, out in enumerate(placed):
            cols = slice(head * HD, (head + 1) * HD)
            for n, fresh in enumerate((new_k, new_v)):
                out[j, n] = jnp.dot(
                    hit, fresh[low:high, cols], preferred_element_type=jnp.float32
                ).astype(jnp.bfloat16)


def place(doc_rows, retrieved, key_new, value_new, positions):
    served, tokens = positions.shape
    width = key_new.shape[1]
    heads = width // HD
    count = served * retrieved
    placed = jax.ShapeDtypeStruct((count, 2, doc_rows, HD), jnp.bfloat16)
    return pl.pallas_call(
        functools.partial(place_kernel, retrieved, doc_rows),
        grid=(served,),
        in_specs=[
            pl.BlockSpec((tokens, width), lambda r: (r, 0)),
            pl.BlockSpec((tokens, width), lambda r: (r, 0)),
            pl.BlockSpec((1, 1, tokens), lambda r: (r, 0, 0)),
        ],
        out_specs=[pl.BlockSpec((retrieved, doc_rows, HD), lambda r: (r, 0, 0))]
        + [pl.BlockSpec((retrieved, 2, doc_rows, HD), lambda r: (r, 0, 0, 0))] * heads,
        out_shape=[jax.ShapeDtypeStruct((count, doc_rows, HD), jnp.bfloat16)] + [placed] * heads,
        compiler_params=pltpu.CompilerParams(vmem_limit_bytes=40 * 2**20),
        cost_estimate=pl.CostEstimate(
            flops=2 * count * doc_rows * 256 * (2 * heads + 1) * HD,
            bytes_accessed=2 * count * doc_rows * (2 * heads + 1) * HD,
            transcendentals=0,
        ),
    )(key_new, value_new, positions[:, None, :])


def attention_kernel(retrieved, doc_rows, tokens, first_doc, slots, lens, *refs):
    docs = refs[:retrieved]
    q_ref, keep, placed, pos_col, o_ref = refs[retrieved : retrieved + 5]
    keys, values, scores, top, total, acc = refs[retrieved + 5 :]
    group = H // KVH
    picks = tokens // retrieved
    span = PAIR * picks
    wide = PAIR * doc_rows
    per_doc = doc_rows // LANES
    factor = HD ** (-0.5) * LOG2E
    block = pl.program_id(0)

    @pl.when(block == 0)
    def blend():
        for j in range(retrieved):
            rows = slice(j * doc_rows, (j + 1) * doc_rows)
            keys[rows, :] = docs[j][0, 0] * keep[j] + placed[j, 0]
            values[rows, :] = docs[j][0, 1] * keep[j] + placed[j, 1]

    top[...] = jnp.full_like(top, MASKED)
    total[...] = jnp.zeros_like(total)
    acc[...] = jnp.zeros_like(acc)
    lane = lax.broadcasted_iota(jnp.int32, (span, LANES), 1)
    half = group // 2
    first_heads = tuple(range(half))
    second_heads = tuple(range(half, group))

    def rows_of(g):
        return slice(g * span, (g + 1) * span)

    def some(heads):
        return slice(heads[0] * span, (heads[-1] + 1) * span)

    def columns_of(n):
        return slice(n * LANES, (n + 1) * LANES)

    def context(ref, p):
        return ref[pl.ds(pl.multiple_of(p * wide, wide), wide), :]

    def score(p, heads):
        query = jnp.concatenate([q_ref[:, columns_of(g)] for g in heads], axis=0)
        raw = lax.dot_general(
            query, context(keys, p), (((1,), (1,)), ((), ())), preferred_element_type=jnp.float32
        )
        limits = []
        for n in range(PAIR):
            doc = p * PAIR + n
            limit = jnp.minimum(pos_col[...] - doc * doc_rows, lens[first_doc + doc] - 1)
            limits.append(jnp.broadcast_to(limit, (span, LANES)))
        best = [top[rows_of(g), :] for g in heads]
        for n in range(wide // LANES):
            mask = lane + (n % per_doc) * LANES <= limits[n // per_doc]
            for at, g in enumerate(heads):
                part = jnp.where(mask, raw[at * span : (at + 1) * span, columns_of(n)], MASKED)
                scores[p, rows_of(g), columns_of(n)] = part
                best[at] = jnp.maximum(best[at], part)
        for at, g in enumerate(heads):
            top[rows_of(g), :] = best[at]

    def settle_top(heads):
        rows = some(heads)
        peak = jnp.max(top[rows, :], axis=1, keepdims=True) * factor
        top[rows, :] = jnp.broadcast_to(peak, (len(heads) * span, LANES))

    def exponent(p, heads):
        for g in heads:
            rows = rows_of(g)
            shift = top[rows, :]
            add = total[rows, :]
            for n in range(wide // LANES):
                expo = jnp.exp2(scores[p, rows, columns_of(n)] * factor - shift)
                scores[p, rows, columns_of(n)] = expo
                add = add + expo
            total[rows, :] = add

    def settle_total(heads):
        rows = some(heads)
        inverse = 1.0 / jnp.sum(total[rows, :], axis=1, keepdims=True)
        total[rows, :] = jnp.broadcast_to(inverse, (len(heads) * span, LANES))

    def combine(p, heads):
        rows = some(heads)
        scale = total[rows, :]
        weights = jnp.concatenate(
            [
                (scores[p, rows, columns_of(n)] * scale).astype(jnp.bfloat16)
                for n in range(wide // LANES)
            ],
            axis=1,
        )
        acc[rows, :] += jnp.dot(weights, context(values, p), preferred_element_type=jnp.float32)

    @pl.loop(0, block + 1)
    def _(p):
        score(p, first_heads)

    settle_top(first_heads)

    @pl.loop(0, block + 1)
    def _(p):
        score(p, second_heads)
        exponent(p, first_heads)

    settle_top(second_heads)
    settle_total(first_heads)

    @pl.loop(0, block + 1)
    def _(p):
        exponent(p, second_heads)
        combine(p, first_heads)

    settle_total(second_heads)

    @pl.loop(0, block + 1)
    def _(p):
        combine(p, second_heads)

    for g in range(group):
        o_ref[:, columns_of(g)] = acc[rows_of(g), :].astype(o_ref.dtype)


def attention(head, request, cache, slots, lens, query, keep, placed, positions):
    served, tokens = positions.shape
    retrieved = slots.shape[0] // served
    doc_rows = cache.shape[2]
    group = H // KVH
    span = tokens // retrieved * PAIR
    blocks = retrieved // PAIR
    rows = group * span
    first_doc = request * retrieved
    doc_specs = [
        pl.BlockSpec(
            (1, 2, doc_rows, HD), lambda b, slots, lens, j=j: (slots[first_doc + j], 0, 0, 0)
        )
        for j in range(retrieved)
    ]
    pairs = tokens * group * retrieved * doc_rows * 5 // 8
    return pl.pallas_call(
        functools.partial(attention_kernel, retrieved, doc_rows, tokens, first_doc),
        grid_spec=pltpu.PrefetchScalarGridSpec(
            num_scalar_prefetch=2,
            grid=(blocks,),
            in_specs=doc_specs
            + [
                pl.BlockSpec((span, group * HD), lambda b, *_: (request * blocks + b, head)),
                pl.BlockSpec((retrieved, doc_rows, HD), lambda b, *_: (request, 0, 0)),
                pl.BlockSpec((retrieved, 2, doc_rows, HD), lambda b, *_: (request, 0, 0, 0)),
                pl.BlockSpec((span, 1), lambda b, *_: (request * blocks + b, 0)),
            ],
            out_specs=pl.BlockSpec((span, group * HD), lambda b, *_: (b, 0)),
            scratch_shapes=[
                pltpu.VMEM((retrieved * doc_rows, HD), jnp.bfloat16),
                pltpu.VMEM((retrieved * doc_rows, HD), jnp.bfloat16),
                pltpu.VMEM((blocks, rows, PAIR * doc_rows), jnp.float32),
                pltpu.VMEM((rows, LANES), jnp.float32),
                pltpu.VMEM((rows, LANES), jnp.float32),
                pltpu.VMEM((rows, HD), jnp.float32),
            ],
        ),
        out_shape=jax.ShapeDtypeStruct((tokens, group * HD), jnp.bfloat16),
        compiler_params=pltpu.CompilerParams(vmem_limit_bytes=48 * 2**20),
        cost_estimate=pl.CostEstimate(
            flops=8 * pairs * HD,
            bytes_accessed=2 * retrieved * doc_rows * 5 * HD,
            transcendentals=pairs,
        ),
    )(
        slots,
        lens,
        *([cache] * retrieved),
        query,
        keep,
        placed,
        positions.reshape(served * tokens, 1),
    )


def body(
    sel_hidden,
    norm_gain,
    w_query,
    w_key,
    w_value,
    w_out,
    doc_cache,
    home,
    doc_ids,
    doc_len,
    positions,
):
    groups = lax.axis_size("grp")
    me = lax.axis_index("grp")
    stored = doc_cache.shape[0]
    doc_rows = doc_cache.shape[2]
    width = doc_cache.shape[3]
    kv_local = width // HD
    group = H // KVH
    served = sel_hidden.shape[0]
    tokens = sel_hidden.shape[1]
    retrieved = doc_ids.shape[1]
    per_group = served * retrieved
    location = home[doc_ids].reshape(groups, per_group)
    owner = location // stored
    slot_index = location % stored
    slots = jnp.arange(per_group, dtype=jnp.int32)
    earlier = (owner[:, :, None] == owner[:, None, :]) & (
        slots[None, None, :] < slots[None, :, None]
    )
    rank = jnp.sum(earlier.astype(jnp.int32), axis=2)
    match = (owner == me)[:, :, None] & (
        rank[:, :, None] == jnp.arange(CAP, dtype=jnp.int32)[None, None, :]
    )
    chosen = jnp.sum(jnp.where(match, slot_index[:, :, None], 0), axis=1)
    own_slots = owner[me] * CAP + rank[me]
    lengths = doc_len[doc_ids.reshape(groups, per_group)[me]]

    incoming = []
    for head in range(kv_local):
        outgoing = pick(head, chosen.reshape(groups * CAP), doc_cache).reshape(
            groups, CAP, 2, doc_rows, HD
        )
        if incoming:
            outgoing, incoming[-1] = lax.optimization_barrier((outgoing, incoming[-1]))
        incoming.append(
            lax.all_to_all(outgoing, "grp", split_axis=0, concat_axis=0, tiled=True)
        )

    xf = sel_hidden.astype(jnp.float32)
    normed = (xf * lax.rsqrt(jnp.mean(xf * xf, axis=-1, keepdims=True) + 1e-05) * norm_gain).astype(
        jnp.bfloat16
    )
    normed_rows = normed.reshape(served * tokens, normed.shape[2])
    query = jnp.dot(normed_rows, w_query, preferred_element_type=jnp.float32).astype(jnp.bfloat16)
    key_new = jnp.dot(normed_rows, w_key, preferred_element_type=jnp.float32).astype(jnp.bfloat16)
    value_new = jnp.dot(normed_rows, w_value, preferred_element_type=jnp.float32).astype(
        jnp.bfloat16
    )

    keep, *placed = place(doc_rows, retrieved, key_new, value_new, positions)
    w_heads = w_out.reshape(-1, kv_local, group * HD, w_out.shape[1])
    mixed = [0.0] * served
    for head in range(kv_local):
        cache = incoming[head].reshape((groups * CAP, 2, doc_rows, HD))
        part = w_heads[:, head].reshape(-1, w_out.shape[1])
        for request in range(served):
            attn = attention(
                head, request, cache, own_slots, lengths, query, keep, placed[head], positions
            )
            gathered = lax.all_gather(attn, "tp", axis=1, tiled=True)
            mixed[request] = mixed[request] + jnp.dot(
                gathered, part, preferred_element_type=jnp.float32
            )
    return jnp.stack(mixed).astype(jnp.bfloat16)


def solution(mesh):
    return jax.shard_map(
        body,
        mesh=mesh,
        in_specs=(
            P("grp", None, None),
            P(),
            P(None, "tp"),
            P(None, "tp"),
            P(None, "tp"),
            P(None, "tp"),
            P("grp", None, None, "tp"),
            P(),
            P(),
            P(),
            P("grp", None),
        ),
        out_specs=P("grp", None, "tp"),
        check_vma=False,
    )
```

```python
import functools

import jax
import jax.numpy as jnp
from jax import lax
from jax.experimental import pallas as pl
from jax.experimental.pallas import tpu as pltpu
from jax.sharding import PartitionSpec as P

H = 32
KVH = 8
HD = 128
CAP = 2
PAIR = 2
LANES = 128
MASKED = -1e30
VMEM_GRANT = 54 * 2**20
LOG2E = 1.4426950408889634


def pick_kernel(chosen, cache, out):
    out[...] = cache[...]


def pick(head, chosen, doc_cache):
    doc_rows = doc_cache.shape[2]
    count = chosen.shape[0]
    return pl.pallas_call(
        pick_kernel,
        grid_spec=pltpu.PrefetchScalarGridSpec(
            num_scalar_prefetch=1,
            grid=(count,),
            in_specs=[pl.BlockSpec((1, 2, doc_rows, HD), lambda i, chosen: (chosen[i], 0, 0, head))],
            out_specs=pl.BlockSpec((1, 2, doc_rows, HD), lambda i, chosen: (i, 0, 0, 0)),
        ),
        out_shape=jax.ShapeDtypeStruct((count, 2, doc_rows, HD), doc_cache.dtype),
        compiler_params=pltpu.CompilerParams(vmem_limit_bytes=VMEM_GRANT),
        cost_estimate=pl.CostEstimate(
            flops=0, bytes_accessed=8 * count * doc_rows * HD, transcendentals=0
        ),
    )(chosen, doc_cache)


def place_kernel(retrieved, doc_rows, new_k, new_v, pos_lane, keep, *placed):
    tokens = new_k.shape[0]
    picks = tokens // retrieved
    for j in range(retrieved):
        low = j * picks // LANES * LANES
        high = min(tokens, -(-(j + 1) * picks // LANES) * LANES)
        at = lax.broadcasted_iota(jnp.int32, (doc_rows, high - low), 0) + j * doc_rows
        hit = jnp.where(at == pos_lane[0, :, low:high], 1.0, 0.0).astype(jnp.bfloat16)
        ones = jnp.ones((high - low, HD), jnp.bfloat16)
        taken = jnp.dot(hit, ones, preferred_element_type=jnp.float32)
        keep[j] = (1.0 - taken).astype(jnp.bfloat16)
        for head, out in enumerate(placed):
            cols = slice(head * HD, (head + 1) * HD)
            for n, fresh in enumerate((new_k, new_v)):
                out[j, n] = jnp.dot(
                    hit, fresh[low:high, cols], preferred_element_type=jnp.float32
                ).astype(jnp.bfloat16)


def place(doc_rows, retrieved, key_new, value_new, positions):
    served, tokens = positions.shape
    width = key_new.shape[1]
    heads = width // HD
    count = served * retrieved
    placed = jax.ShapeDtypeStruct((count, 2, doc_rows, HD), jnp.bfloat16)
    return pl.pallas_call(
        functools.partial(place_kernel, retrieved, doc_rows),
        grid=(served,),
        in_specs=[
            pl.BlockSpec((tokens, width), lambda r: (r, 0)),
            pl.BlockSpec((tokens, width), lambda r: (r, 0)),
            pl.BlockSpec((1, 1, tokens), lambda r: (r, 0, 0)),
        ],
        out_specs=[pl.BlockSpec((retrieved, doc_rows, HD), lambda r: (r, 0, 0))]
        + [pl.BlockSpec((retrieved, 2, doc_rows, HD), lambda r: (r, 0, 0, 0))] * heads,
        out_shape=[jax.ShapeDtypeStruct((count, doc_rows, HD), jnp.bfloat16)] + [placed] * heads,
        compiler_params=pltpu.CompilerParams(vmem_limit_bytes=VMEM_GRANT),
        cost_estimate=pl.CostEstimate(
            flops=2 * count * doc_rows * 256 * (2 * heads + 1) * HD,
            bytes_accessed=2 * count * doc_rows * (2 * heads + 1) * HD,
            transcendentals=0,
        ),
    )(key_new, value_new, positions[:, None, :])


def attention_kernel(retrieved, doc_rows, tokens, slots, lens, *refs):
    docs = refs[:retrieved]
    q_ref, keep, placed, pos_col, o_ref = refs[retrieved : retrieved + 5]
    keys, values, scores = refs[retrieved + 5 :]
    group = H // KVH
    picks = tokens // retrieved
    span = PAIR * picks
    wide = PAIR * doc_rows
    per_doc = doc_rows // LANES
    factor = HD ** (-0.5) * LOG2E
    first_doc = pl.program_id(0) * retrieved
    block = pl.program_id(1)
    half = group // 2
    first_heads = tuple(range(half))
    second_heads = tuple(range(half, group))

    @pl.when(block == 0)
    def blend():
        for j in range(retrieved):
            rows = slice(j * doc_rows, (j + 1) * doc_rows)
            keys[:, rows] = (docs[j][0, 0] * keep[j] + placed[j, 0]).T
            values[rows, :] = docs[j][0, 1] * keep[j] + placed[j, 1]

    def rows_of(g):
        return slice(g * span, (g + 1) * span)

    def some(heads):
        return slice(heads[0] * span, (heads[-1] + 1) * span)

    def columns_of(n):
        return slice(n * LANES, (n + 1) * LANES)

    def run(last):
        top, total, acc = {}, {}, {}

        def score(p, heads):
            query = jnp.concatenate([q_ref[:, columns_of(g)] for g in heads], axis=0)
            raw = jnp.dot(
                query, keys[:, p * wide : (p + 1) * wide], preferred_element_type=jnp.float32
            )
            for n in range(wide // LANES):
                doc = p * PAIR + n // per_doc
                limit = lens[first_doc + doc] - 1
                if p == last:
                    limit = jnp.minimum(pos_col[...] - doc * doc_rows, limit)
                rows = span if p == last else 1
                lane = lax.broadcasted_iota(jnp.int32, (rows, LANES), 1)
                mask = lane + (n % per_doc) * LANES <= limit
                for at, g in enumerate(heads):
                    part = jnp.where(mask, raw[at * span : (at + 1) * span, columns_of(n)], MASKED)
                    scores[p, rows_of(g), columns_of(n)] = part
                    top[g] = jnp.maximum(top[g], part) if g in top else part

        def settle_top(heads):
            for g in heads:
                top[g] = jnp.max(top[g], axis=1, keepdims=True) * factor

        def exponent(p, heads):
            for g in heads:
                for n in range(wide // LANES):
                    expo = jnp.exp2(scores[p, rows_of(g), columns_of(n)] * factor - top[g])
                    scores[p, rows_of(g), columns_of(n)] = expo
                    total[g] = total[g] + expo if g in total else expo

        def settle_total(heads):
            for g in heads:
                total[g] = 1.0 / jnp.sum(total[g], axis=1, keepdims=True)

        def combine(p, heads):
            weights = jnp.concatenate(
                [
                    (scores[p, rows_of(g), :] * total[g]).astype(jnp.bfloat16)
                    for g in heads
                ],
                axis=0,
            )
            term = jnp.dot(
                weights, values[p * wide : (p + 1) * wide, :], preferred_element_type=jnp.float32
            )
            acc[heads] = acc[heads] + term if heads in acc else term

        def finish(heads):
            for at, g in enumerate(heads):
                o_ref[:, columns_of(g)] = acc[heads][at * span : (at + 1) * span].astype(o_ref.dtype)

        pairs = range(last + 1)
        for p in pairs:
            score(p, first_heads)
        settle_top(first_heads)
        for p in pairs:
            score(p, second_heads)
            exponent(p, first_heads)
        settle_top(second_heads)
        settle_total(first_heads)
        for p in pairs:
            exponent(p, second_heads)
            combine(p, first_heads)
        finish(first_heads)
        settle_total(second_heads)
        for p in pairs:
            combine(p, second_heads)
        finish(second_heads)

    for last in range(retrieved // PAIR):
        pl.when(block == last)(functools.partial(run, last))


def attention(head, cache, slots, lens, query, keep, placed, positions):
    served, tokens = positions.shape
    retrieved = slots.shape[0] // served
    doc_rows = cache.shape[2]
    group = H // KVH
    span = tokens // retrieved * PAIR
    blocks = retrieved // PAIR
    rows = group * span
    doc_specs = [
        pl.BlockSpec(
            (1, 2, doc_rows, HD),
            lambda r, b, slots, lens, j=j: (slots[r * retrieved + j], 0, 0, 0),
        )
        for j in range(retrieved)
    ]
    pairs = served * tokens * group * retrieved * doc_rows * 5 // 8
    return pl.pallas_call(
        functools.partial(attention_kernel, retrieved, doc_rows, tokens),
        grid_spec=pltpu.PrefetchScalarGridSpec(
            num_scalar_prefetch=2,
            grid=(served, blocks),
            in_specs=doc_specs
            + [
                pl.BlockSpec((span, group * HD), lambda r, b, *_: (r * blocks + b, head)),
                pl.BlockSpec((retrieved, doc_rows, HD), lambda r, b, *_: (r, 0, 0)),
                pl.BlockSpec((retrieved, 2, doc_rows, HD), lambda r, b, *_: (r, 0, 0, 0)),
                pl.BlockSpec((span, 1), lambda r, b, *_: (r * blocks + b, 0)),
            ],
            out_specs=pl.BlockSpec((span, group * HD), lambda r, b, *_: (r * blocks + b, 0)),
            scratch_shapes=[
                pltpu.VMEM((HD, retrieved * doc_rows), jnp.bfloat16),
                pltpu.VMEM((retrieved * doc_rows, HD), jnp.bfloat16),
                pltpu.VMEM((blocks, rows, PAIR * doc_rows), jnp.float32),
            ],
        ),
        out_shape=jax.ShapeDtypeStruct((served * tokens, group * HD), jnp.bfloat16),
        compiler_params=pltpu.CompilerParams(vmem_limit_bytes=VMEM_GRANT),
        cost_estimate=pl.CostEstimate(
            flops=8 * pairs * HD,
            bytes_accessed=2 * served * retrieved * doc_rows * 5 * HD,
            transcendentals=pairs,
        ),
    )(
        slots,
        lens,
        *([cache] * retrieved),
        query,
        keep,
        placed,
        positions.reshape(served * tokens, 1),
    )


def chained_product(attn, w_out, head, kv_local):
    size = lax.axis_size("tp")
    at = lax.axis_index("tp")
    depth = attn.shape[1]

    def rows_for(step):
        shard = lax.rem(at - step + size, size)
        return lax.dynamic_slice_in_dim(w_out, (shard * kv_local + head) * depth, depth, 0)

    def product(block, step):
        return jnp.dot(block, rows_for(step), preferred_element_type=jnp.float32)

    right, left = [attn], [attn]
    for step in range(1, size):
        up = [(n, n + 1) for n in range(step - 1, size - 1)]
        right.append(lax.ppermute(right[-1], "tp", up))
        left.append(lax.ppermute(left[-1], "tp", [(size - 1 - a, size - 1 - b) for a, b in up]))
    out = product(attn, 0)
    for step in sorted(range(1, size), key=lambda n: max(n, size - n)):
        out = out + product(right[step] + left[size - step], step)
    return out


def body(
    sel_hidden,
    norm_gain,
    w_query,
    w_key,
    w_value,
    w_out,
    doc_cache,
    home,
    doc_ids,
    doc_len,
    positions,
):
    groups = lax.axis_size("grp")
    me = lax.axis_index("grp")
    stored = doc_cache.shape[0]
    doc_rows = doc_cache.shape[2]
    width = doc_cache.shape[3]
    kv_local = width // HD
    group = H // KVH
    served = sel_hidden.shape[0]
    tokens = sel_hidden.shape[1]
    retrieved = doc_ids.shape[1]
    per_group = served * retrieved
    location = home[doc_ids].reshape(groups, per_group)
    owner = location // stored
    slot_index = location % stored
    slots = jnp.arange(per_group, dtype=jnp.int32)
    earlier = (owner[:, :, None] == owner[:, None, :]) & (
        slots[None, None, :] < slots[None, :, None]
    )
    rank = jnp.sum(earlier.astype(jnp.int32), axis=2)
    match = (owner == me)[:, :, None] & (
        rank[:, :, None] == jnp.arange(CAP, dtype=jnp.int32)[None, None, :]
    )
    chosen = jnp.sum(jnp.where(match, slot_index[:, :, None], 0), axis=1)
    own_slots = owner[me] * CAP + rank[me]
    lengths = doc_len[doc_ids.reshape(groups, per_group)[me]]

    incoming = []
    for head in range(kv_local):
        outgoing = pick(head, chosen.reshape(groups * CAP), doc_cache).reshape(
            groups, CAP, 2, doc_rows, HD
        )
        if incoming:
            outgoing, incoming[-1] = lax.optimization_barrier((outgoing, incoming[-1]))
        incoming.append(
            lax.all_to_all(outgoing, "grp", split_axis=0, concat_axis=0, tiled=True)
        )

    xf = sel_hidden.astype(jnp.float32)
    normed = (xf * lax.rsqrt(jnp.mean(xf * xf, axis=-1, keepdims=True) + 1e-05) * norm_gain).astype(
        jnp.bfloat16
    )
    normed_rows = normed.reshape(served * tokens, normed.shape[2])
    query = jnp.dot(normed_rows, w_query, preferred_element_type=jnp.float32).astype(jnp.bfloat16)
    key_new = jnp.dot(normed_rows, w_key, preferred_element_type=jnp.float32).astype(jnp.bfloat16)
    value_new = jnp.dot(normed_rows, w_value, preferred_element_type=jnp.float32).astype(
        jnp.bfloat16
    )

    keep, *placed = place(doc_rows, retrieved, key_new, value_new, positions)
    w_heads = w_out.reshape(-1, kv_local, group * HD, w_out.shape[1])
    mixed = 0.0
    for head in range(kv_local):
        cache = incoming[head].reshape((groups * CAP, 2, doc_rows, HD))
        attn = attention(
            head, cache, own_slots, lengths, query, keep, placed[head], positions
        )
        if head < kv_local - 1:
            gathered = lax.all_gather(attn, "tp", axis=1, tiled=True)
            part = w_heads[:, head].reshape(-1, w_out.shape[1])
            mixed = mixed + jnp.dot(gathered, part, preferred_element_type=jnp.float32)
        else:
            mixed = mixed + chained_product(attn, w_out, head, kv_local)
    return mixed.astype(jnp.bfloat16).reshape(served, tokens, w_out.shape[1])


def solution(mesh):
    return jax.shard_map(
        body,
        mesh=mesh,
        in_specs=(
            P("grp", None, None),
            P(),
            P(None, "tp"),
            P(None, "tp"),
            P(None, "tp"),
            P(None, "tp"),
            P("grp", None, None, "tp"),
            P(),
            P(),
            P(),
            P("grp", None),
        ),
        out_specs=P("grp", None, "tp"),
        check_vma=False,
    )
```
